32 devices in a mesh: leaf: 8 (over z, y), cols: 4 (over x, core).
Axes of the slice: x: 2, y: 2, z: 4, core: 2. Of those that a mesh axis runs over, the one named last changes fastest.
Arguments:
- points: bfloat16 [32768, 64], P('leaf', 'cols'), may hold values from -6 to 6
- weights: bfloat16 [32768, 1024], P('leaf', 'cols'), may hold values from -6 to 6
- leaf_basis: bfloat16 [8192, 1024], P('leaf'), may hold values from -0.1875 to 0.1875
- dev_transfer: bfloat16 [2048, 1024], P('leaf'), may hold values from -0.1875 to 0.1875
- group_transfer: bfloat16 [512, 1024], P('leaf'), may hold values from -0.1875 to 0.1875
- leaf_skeleton: int32 [32, 256], P('leaf'), may hold values from 0 to 1023, as said below
- dev_skeleton: int32 [8, 256], P('leaf'), may hold values from 0 to 1023, as said below
- group_skeleton: int32 [2, 256], replicated, may hold values from 0 to 1023, as said below
- near_list: int32 [32, 3], P('leaf'), may hold values from 0 to 31, as said below
- near_count: int32 [32], P('leaf'), may hold values from 1 to 3
Outputs:
- potentials: float32 [32768, 1024], P('leaf', 'cols')
The draws below stay inside these ranges and needn't reach their ends.
Inputs may be any that keep to these rules, and one draw needn't show every extreme that they name: `leaf_skeleton`: each row holds 256 distinct point numbers within the leaf. `dev_skeleton`: each row holds 256 distinct numbers into the 1024 skeleton points of the node's children, in child order. `group_skeleton`: each row holds 256 distinct numbers into the 1024 skeleton points of the node's children, in child order. `near_list`: row l names leaves of the first-level node holding leaf l and of the first-level nodes just before and after it; its first entry is l itself and its first near_count[l] entries are distinct; later entries are leaf numbers that are not used.
All inputs are finite; a program needn't handle non-finite values.
Results may differ from the reference program's by a relative error of at most 0.005.
Values may be sent and summed in bfloat16 or wider, within the bound.
A program may use at most 128 MiB of HBM per device.

```python
import jax
import jax.numpy as jnp
from jax import lax

DIM = 64
COLS = 1024
RANK = 256
LEAF = 1024
LD = 4
NEARMAX = 3
LEAVES = 32
NPTS = 32768
GROUPS = 2
N_LEAF = 8


def pick_rows(key, row_count, choices_of, kept):
    scores = jax.random.randint(key, (row_count, choices_of), 0, 1 << 20) * choices_of + jnp.arange(choices_of, dtype=jnp.int32)[None, :]
    ordering = jnp.argsort(scores, axis=1, stable=True)
    return ordering[:, :kept].astype(jnp.int32)


def draw_leaf_skeleton(key, part):
    return pick_rows(jax.random.fold_in(key, 11), LD * N_LEAF, LEAF, RANK)


def draw_dev_skeleton(key, part):
    return pick_rows(jax.random.fold_in(key, 12), N_LEAF, LD * RANK, RANK)


def draw_group_skeleton(key, part):
    return pick_rows(jax.random.fold_in(key, 13), N_LEAF // LD, LD * RANK, RANK)


def near_tables(key):
    leaves = LD * N_LEAF
    key_order, key_count = jax.random.split(jax.random.fold_in(key, 21))
    leaf_ids = jnp.arange(leaves, dtype=jnp.int32)
    block_ids = leaf_ids // LD
    slot_ids = leaf_ids % LD
    offsets = jnp.arange(3 * LD, dtype=jnp.int32)
    candidates = (block_ids[:, None] - 1) * LD + offsets[None, :]
    valid_mask = (candidates >= 0) & (candidates < leaves) & (candidates != leaf_ids[:, None])
    forced_pick = (slot_ids[:, None] == LD - 1) & (candidates == (block_ids[:, None] + 1) * LD) | (slot_ids[:, None] == 0) & (candidates == block_ids[:, None] * LD - 1)
    forced_pick = forced_pick & valid_mask
    scores = jax.random.randint(key_order, (leaves, 3 * LD), 0, 1 << 16) * (4 * LD) + offsets[None, :]
    scores = jnp.where(valid_mask, scores, scores + (1 << 24))
    scores = jnp.where(forced_pick, -1, scores)
    ordering = jnp.argsort(scores, axis=1, stable=True)
    chosen = jnp.take_along_axis(candidates, ordering, axis=1)[:, :NEARMAX - 1]
    near_table = jnp.concatenate([leaf_ids[:, None], chosen], axis=1).astype(jnp.int32)
    near_len = jax.random.randint(key_count, (leaves,), 1, NEARMAX + 1)
    near_len = jnp.where(jnp.any(forced_pick, axis=1), jnp.maximum(near_len, 2), near_len)
    near_len = jnp.where(leaf_ids == 1, NEARMAX, near_len)
    near_len = jnp.where(leaf_ids == 2, 1, near_len)
    return (near_table, near_len.astype(jnp.int32))


def draw_near_list(key, part):
    return near_tables(key)[0]


def draw_near_count(key, part):
    return near_tables(key)[1]


def levels(own_key, dims, shards, low, high):
    factor_of = 1.0
    for dim, blocks in shards:
        steps = jax.random.uniform(jax.random.fold_in(jax.random.fold_in(own_key, 6), dim), (blocks,), jnp.float32, low / len(shards), high / len(shards))
        factor_of = factor_of * jnp.repeat(jnp.exp(steps), dims[dim] // blocks).reshape((-1,) + (1,) * (len(dims) - 1 - dim))
    return factor_of


def gaussian(own_key, shape, spread, bound, pieces=(), kind=jnp.bfloat16):
    values = spread * jax.random.normal(own_key, shape, jnp.float32)
    if pieces:
        values = values * levels(own_key, shape, pieces, -0.22, 0.18)
    return jnp.clip(values, -bound, bound).astype(kind)


def setup_inputs(seed: int = 0) -> dict:
    key_of = jax.random.split(jax.random.key(seed), 11)
    points = gaussian(key_of[0], (NPTS, DIM), 1.0, 6.0, ((0, 8), (1, 4)))
    weights = gaussian(key_of[1], (NPTS, COLS), 1.0, 6.0, ((0, 8), (1, 4)))
    leaf_basis = gaussian(key_of[2], (LEAVES * RANK, LEAF), LEAF ** -0.5, 0.1875, ((0, 8),))
    dev_transfer = gaussian(key_of[3], (N_LEAF * RANK, LD * RANK), (LD * RANK) ** -0.5, 0.1875, ((0, 8),))
    group_transfer = gaussian(key_of[4], (GROUPS * RANK, LD * RANK), (LD * RANK) ** -0.5, 0.1875, ((0, 8),))
    leaf_skeleton = draw_leaf_skeleton(jax.random.fold_in(key_of[10], 71), 0)
    dev_skeleton = draw_dev_skeleton(jax.random.fold_in(key_of[10], 71), 0)
    group_skeleton = draw_group_skeleton(jax.random.fold_in(key_of[10], 71), 0)
    near_list = draw_near_list(jax.random.fold_in(key_of[10], 71), 0)
    near_count = draw_near_count(jax.random.fold_in(key_of[10], 71), 0)
    return {"points": points, "weights": weights, "leaf_basis": leaf_basis, "dev_transfer": dev_transfer, "group_transfer": group_transfer, "leaf_skeleton": leaf_skeleton, "dev_skeleton": dev_skeleton, "group_skeleton": group_skeleton, "near_list": near_list, "near_count": near_count}


SHARPNESS = 2.0


def product(left_side, right_side):
    return jnp.dot(left_side.astype(jnp.float32), right_side.astype(jnp.float32), precision=lax.Precision.HIGHEST)


def kernel_matrix(row_points, col_points):
    row_float = row_points.astype(jnp.float32)
    col_float = col_points.astype(jnp.float32)
    inner_prod = jnp.dot(row_float, col_float.T, precision=lax.Precision.HIGHEST)
    row_norms = jnp.sum(row_float * row_float, axis=1)
    col_norms = jnp.sum(col_float * col_float, axis=1)
    return jnp.exp((-SHARPNESS / row_points.shape[1]) * (row_norms[:, None] + col_norms[None, :] - 2.0 * inner_prod))


def sibling_term(coords, skeleton_vals, skel_rank):
    blocks = jnp.arange(coords.shape[0], dtype=jnp.int32) // skel_rank
    coupling = jnp.where(blocks[:, None] != blocks[None, :], kernel_matrix(coords, coords), 0.0).astype(jnp.bfloat16)
    return product(coupling, skeleton_vals)


def reference(points, weights, leaf_basis, dev_transfer, group_transfer, leaf_skeleton, dev_skeleton, group_skeleton, near_list, near_count):
    leaves = LD * N_LEAF
    groups = N_LEAF // LD
    leaf_points = points.reshape(leaves, LEAF, DIM)
    leaf_weights = weights.reshape(leaves, LEAF, COLS)
    leaf_maps = leaf_basis.reshape(leaves, RANK, LEAF)
    leaf_skel = jnp.einsum('lrp,lpc->lrc', leaf_maps.astype(jnp.float32), leaf_weights.astype(jnp.float32), precision=lax.Precision.HIGHEST).astype(jnp.bfloat16)
    leaf_coords = jnp.take_along_axis(leaf_points, leaf_skeleton[:, :, None], axis=1)

    def node_level(items):
        skeleton_vals, coords, transfer, chosen = items
        field = sibling_term(coords, skeleton_vals, RANK)
        return field, product(transfer, skeleton_vals).astype(jnp.bfloat16), jnp.take(coords, chosen, axis=0)

    leaf_field, node_skel, node_coords = lax.map(node_level, (leaf_skel.reshape(N_LEAF, LD * RANK, COLS), leaf_coords.reshape(N_LEAF, LD * RANK, DIM), dev_transfer.reshape(N_LEAF, RANK, LD * RANK), dev_skeleton))
    node_field, group_skel, group_coords = lax.map(node_level, (node_skel.reshape(groups, LD * RANK, COLS), node_coords.reshape(groups, LD * RANK, DIM), group_transfer.reshape(groups, RANK, LD * RANK), group_skeleton))
    top_field = sibling_term(group_coords.reshape(groups * RANK, DIM), group_skel.reshape(groups * RANK, COLS), RANK).astype(jnp.bfloat16)
    node_down = jnp.einsum('grk,grc->gkc', group_transfer.reshape(groups, RANK, LD * RANK).astype(jnp.float32), top_field.reshape(groups, RANK, COLS).astype(jnp.float32), precision=lax.Precision.HIGHEST)
    node_total = (node_field + node_down).astype(jnp.bfloat16)
    leaf_down = jnp.einsum('drk,drc->dkc', dev_transfer.reshape(N_LEAF, RANK, LD * RANK).astype(jnp.float32), node_total.reshape(N_LEAF, RANK, COLS).astype(jnp.float32), precision=lax.Precision.HIGHEST)
    leaf_total = (leaf_field + leaf_down).astype(jnp.bfloat16).reshape(leaves, RANK, COLS)

    def finish(items):
        leaf_no, leaf_map, field, near_row, near_len = items
        far_part = product(leaf_map.T, field)
        near_sum = jnp.zeros((LEAF, COLS), jnp.float32)
        for slot_no in range(NEARMAX):
            def add_tile(source):
                block = kernel_matrix(leaf_points[leaf_no], leaf_points[source]).astype(jnp.bfloat16)
                return product(block, leaf_weights[source])

            def no_tile(source):
                return jnp.zeros((LEAF, COLS), jnp.float32)

            near_sum = near_sum + lax.cond(slot_no < near_len, add_tile, no_tile, near_row[slot_no])
        return near_sum + far_part

    result = lax.map(finish, (jnp.arange(leaves, dtype=jnp.int32), leaf_maps, leaf_total, near_list, near_count))
    return result.reshape(leaves * LEAF, COLS)
```

```python
import functools
import math

import jax
import jax.numpy as jnp
from jax import lax
from jax.experimental import pallas as pl
from jax.experimental.pallas import tpu as pltpu
from jax.sharding import PartitionSpec as P

LEAF = 1024
CHILDREN = 4
SHARPNESS = 2.0
F32 = jnp.float32
BF16 = jnp.bfloat16
VMEM_LIMIT = 48 << 20


def mm(a, b):
    return jnp.dot(a, b, preferred_element_type=F32)


def mm_t(a, b):
    return lax.dot_general(a, b, (((0,), (0,)), ((), ())), preferred_element_type=F32)


def augmented(coords, left):
    wide = coords.astype(F32)
    half = -0.5 * jnp.sum(wide * wide, axis=0, keepdims=True)
    high = half.astype(BF16).astype(F32)
    rest = half - high
    mid = rest.astype(BF16).astype(F32)
    low = rest - mid
    row = lax.broadcasted_iota(jnp.int32, coords.shape, 0)
    at, ones = (0, 3) if left else (3, 0)
    extra = jnp.where((row >= ones) & (row < ones + 3), 1.0, 0.0)
    for k, piece in enumerate((high, mid, low)):
        extra = jnp.where(row == at + k, piece, extra)
    return jnp.concatenate([coords, extra.astype(BF16)], axis=0)


def kernel_of(inner, feat):
    return jnp.exp2(inner * (2.0 * SHARPNESS / feat * math.log2(math.e))).astype(BF16)


def pick(coords, index_row, offset=0):
    n = coords.shape[1]
    place = lax.broadcasted_iota(jnp.int32, (n, index_row.shape[1]), 0)
    hot = jnp.where(place == index_row - offset, 1.0, 0.0).astype(BF16)
    return mm(coords, hot)


def leaf_kernel(pts_ref, w_ref, basis_ref, dev_ref, lskel_ref, dskel_ref, field_ref, packed_ref, skel_ref):
    feat = pts_ref.shape[0]
    leaves, rank = lskel_ref.shape
    coords = []
    for l in range(leaves):
        skel_ref[pl.ds(l * rank, rank), :] = mm(
            basis_ref[pl.ds(l * rank, rank), :], w_ref[pl.ds(l * LEAF, LEAF), :]
        ).astype(BF16)
        coords.append(pick(pts_ref[:, pl.ds(l * LEAF, LEAF)], lskel_ref[pl.ds(l, 1), :]).astype(BF16))
    packed_ref[:rank, :] = mm(dev_ref[...], skel_ref[...]).astype(BF16)
    packed_ref[rank:, :] = pick(jnp.concatenate(coords, axis=1), dskel_ref[...]).astype(BF16)
    rights = [augmented(c, False) for c in coords]
    for l in range(leaves):
        left = augmented(coords[l], True).T
        total = None
        for o in range(leaves):
            if o != l:
                term = mm(kernel_of(mm(left, rights[o]), feat), skel_ref[pl.ds(o * rank, rank), :])
                total = term if total is None else total + term
        field_ref[pl.ds(l * rank, rank), :] = total


def node_kernel(pos_ref, *refs):
    packs = refs[:CHILDREN]
    transfers = refs[CHILDREN : 2 * CHILDREN]
    gskel_ref, field_ref, group_ref = refs[2 * CHILDREN :]
    member = lax.rem(pos_ref[0], CHILDREN)
    group = pos_ref[0] // CHILDREN
    rank = field_ref.shape[0]
    feat = packs[0].shape[0] - rank
    quarter = transfers[0].shape[0]
    children = [member ^ f for f in range(CHILDREN)]
    for q in range(CHILDREN):
        total = None
        for f in range(CHILDREN):
            cols = pl.ds(pl.multiple_of(children[f] * rank, rank), rank)
            term = mm(transfers[q][:, cols], packs[f][:rank, :])
            total = term if total is None else total + term
        group_ref[pl.ds(pl.multiple_of(children[q] * quarter, quarter), quarter), :] = total.astype(BF16)
    chosen = gskel_ref[pl.ds(group, 1), :]
    coords = None
    for f in range(CHILDREN):
        term = pick(packs[f][rank:, :], chosen, children[f] * rank)
        coords = term if coords is None else coords + term
    group_ref[rank:, :] = coords.astype(BF16)
    left = augmented(packs[0][rank:, :], True).T
    total = None
    for f in range(1, CHILDREN):
        term = mm(kernel_of(mm(left, augmented(packs[f][rank:, :], False)), feat), packs[f][:rank, :])
        total = term if total is None else total + term
    field_ref[...] = total


def top_kernel(others, pos_ref, *refs):
    own_ref = refs[0]
    other_refs = refs[1 : 1 + others]
    transfers = refs[1 + others : 1 + others + CHILDREN]
    nfield_ref, lfield_ref, dev_ref, out_ref, top_ref = refs[1 + others + CHILDREN :]
    rank = nfield_ref.shape[0]
    feat = own_ref.shape[0] - rank
    quarter = transfers[0].shape[0]
    member = lax.rem(pos_ref[0], CHILDREN)
    left = augmented(own_ref[rank:, :], True).T
    total = jnp.zeros(nfield_ref.shape, F32)
    for ref in other_refs:
        total += mm(kernel_of(mm(left, augmented(ref[rank:, :], False)), feat), ref[:rank, :])
    top_ref[...] = total.astype(BF16)
    shares = nfield_ref[...]
    cols = pl.ds(pl.multiple_of(member * rank, rank), rank)
    for f in range(CHILDREN):
        rows = pl.ds(pl.multiple_of((member ^ f) * quarter, quarter), quarter)
        shares += mm_t(transfers[f][:, cols], top_ref[rows, :])
    node_total = shares.astype(BF16)
    out_ref[...] = (lfield_ref[...] + mm_t(dev_ref[...], node_total)).astype(BF16)


def near_kernel(first, far, info_ref, count_ref, list_ref, *refs):
    refs = list(refs)
    own_ref, pts_ref = refs[:2]
    w_refs = refs[2 : 2 + info_ref.shape[0] - 1]
    refs = refs[2 + len(w_refs) :]
    acc_ref = None if first else refs.pop(0)
    if far:
        basis_ref, total_ref = refs.pop(0), refs.pop(0)
    out_ref, left_ref = refs
    leaf = pl.program_id(0)
    feat = own_ref.shape[0]
    slots = list_ref.shape[1]
    chunk = 256
    per = w_refs[0].shape[0] // LEAF
    left_ref[...] = augmented(own_ref[...], True).T
    if first:
        out_ref[...] = jnp.zeros_like(out_ref)
    elif far:
        out_ref[...] = acc_ref[...] + mm_t(basis_ref[...], total_ref[...])
    else:
        out_ref[...] = acc_ref[...]
    for slot in range(slots):
        source = list_ref[leaf, slot]
        for part, w_ref in enumerate(w_refs):
            place = source - info_ref[part]

            @pl.when((slot < count_ref[leaf]) & (place >= 0) & (place < per))
            def _():
                at = pl.multiple_of((part * per + place) * LEAF, LEAF)
                right = augmented(pts_ref[:, pl.ds(at, LEAF)], False)
                rows = pl.ds(pl.multiple_of(place * LEAF, LEAF), LEAF)
                for r in range(0, LEAF, chunk):
                    block = kernel_of(mm(left_ref[pl.ds(r, chunk), :], right), feat)
                    out_ref[pl.ds(r, chunk), :] += mm(block, w_ref[rows, :])


def whole():
    return pl.BlockSpec(memory_space=pltpu.VMEM)


def scalar():
    return pl.BlockSpec(memory_space=pltpu.SMEM)


def cost(flops, nbytes):
    return pl.CostEstimate(flops=int(flops), bytes_accessed=int(nbytes), transcendentals=0)


def near_call(info, near_count, near_list, own_pts, pts, parts, acc, basis, total, pairs):
    feat, rows = own_pts.shape
    width = parts[0].shape[1]
    leaves = rows // LEAF
    const = lambda l, *_: (0, 0)
    args = [own_pts, pts, *parts]
    specs = [pl.BlockSpec((feat, LEAF), lambda l, *_: (0, l)), pl.BlockSpec(pts.shape, const)]
    specs += [pl.BlockSpec(p.shape, const) for p in parts]
    alias = {}
    if acc is not None:
        alias = {3 + len(args): 0}
        args.append(acc)
        specs.append(pl.BlockSpec((LEAF, width), lambda l, *_: (l, 0)))
    if basis is not None:
        rank = basis.shape[0] // leaves
        args += [basis, total]
        specs += [
            pl.BlockSpec((rank, LEAF), lambda l, *_: (l, 0)),
            pl.BlockSpec((rank, width), lambda l, *_: (l, 0)),
        ]
    return pl.pallas_call(
        functools.partial(near_kernel, acc is None, basis is not None),
        grid_spec=pltpu.PrefetchScalarGridSpec(
            num_scalar_prefetch=3,
            grid=(leaves,),
            in_specs=specs,
            out_specs=pl.BlockSpec((LEAF, width), lambda l, *_: (l, 0)),
            scratch_shapes=[pltpu.VMEM((LEAF, 2 * feat), BF16)],
        ),
        out_shape=jax.ShapeDtypeStruct((rows, width), F32),
        input_output_aliases=alias,
        compiler_params=pltpu.CompilerParams(vmem_limit_bytes=VMEM_LIMIT),
        cost_estimate=cost(pairs * 1.8e9, 8 << 20),
    )(info, near_count, near_list, *args)


def per_device(
    points,
    weights,
    leaf_basis,
    dev_transfer,
    group_transfer,
    leaf_skeleton,
    dev_skeleton,
    group_skeleton,
    near_list,
    near_count,
):
    size = lax.axis_size("leaf")
    position = lax.axis_index("leaf")
    rows, width = weights.shape
    leaves = rows // LEAF
    rank = leaf_skeleton.shape[1]
    groups = size // CHILDREN

    def flipped(value, mask):
        return lax.ppermute(value, "leaf", [(i, i ^ mask) for i in range(size)])

    def relayed(value):
        pairs = [(i, i + 2) for i in range(0, size - 2, 2)]
        pairs += [(i, i - 2) for i in range(3, size, 2)]
        return lax.ppermute(value, "leaf", pairs)

    own_slice = points.T
    own_pts = lax.all_gather(own_slice, "cols", axis=0, tiled=True)
    swap_slice = flipped(own_slice, 1)
    relay_slice = relayed(swap_slice)
    transfers = [group_transfer] + [flipped(group_transfer, f) for f in range(1, CHILDREN)]
    halves = 2
    step = rows // halves
    swap_w = [flipped(weights[h * step : (h + 1) * step], 1) for h in range(halves)]
    relay_w = [relayed(part) for part in swap_w]
    swap_pts = lax.all_gather(swap_slice, "cols", axis=0, tiled=True)
    relay_pts = lax.all_gather(relay_slice, "cols", axis=0, tiled=True)

    feat = own_pts.shape[0]
    params = pltpu.CompilerParams(vmem_limit_bytes=VMEM_LIMIT)
    leaf_field, packed = pl.pallas_call(
        leaf_kernel,
        out_shape=(
            jax.ShapeDtypeStruct((leaves * rank, width), F32),
            jax.ShapeDtypeStruct((rank + feat, width), BF16),
        ),
        in_specs=[whole()] * 6,
        out_specs=(whole(), whole()),
        scratch_shapes=[pltpu.VMEM((leaves * rank, width), BF16)],
        compiler_params=params,
        cost_estimate=cost(5e9, 6 << 20),
    )(own_pts, weights, leaf_basis, dev_transfer, leaf_skeleton, dev_skeleton)
    packs = [packed] + [flipped(packed, f) for f in range(1, CHILDREN)]
    pos = position.astype(jnp.int32)[None]
    node_field, group = pl.pallas_call(
        node_kernel,
        out_shape=(
            jax.ShapeDtypeStruct((rank, width), F32),
            jax.ShapeDtypeStruct((rank + feat, width), BF16),
        ),
        in_specs=[scalar()] + [whole()] * (2 * CHILDREN + 1),
        out_specs=(whole(), whole()),
        compiler_params=params,
        cost_estimate=cost(2e9, 2 << 20),
    )(pos, *packs, *transfers, group_skeleton)
    others = [
        lax.ppermute(group, "leaf", [(i, (i + CHILDREN * k) % size) for i in range(size)])
        for k in range(1, groups)
    ]
    leaf_total = pl.pallas_call(
        functools.partial(top_kernel, len(others)),
        out_shape=jax.ShapeDtypeStruct((leaves * rank, width), BF16),
        in_specs=[scalar()] + [whole()] * (len(others) + CHILDREN + 4),
        out_specs=whole(),
        scratch_shapes=[pltpu.VMEM((rank, width), BF16)],
        compiler_params=params,
        cost_estimate=cost(2e9, 3 << 20),
    )(pos, group, *others, *transfers, node_field, leaf_field, dev_transfer)

    per = leaves // halves
    counts = near_count.astype(jnp.int32)
    edges = jnp.arange(halves + 1, dtype=jnp.int32) * per
    beyond = jnp.where(position % 2 == 0, position - 1, position + 1)
    near = functools.partial(near_call, near_count=counts, near_list=near_list, own_pts=own_pts)
    own_edges = jnp.arange(2, dtype=jnp.int32) * leaves
    acc = near(own_edges + position * leaves, pts=own_pts, parts=[weights], acc=None, basis=None, total=None, pairs=6)
    acc = near(edges + (position ^ 1) * leaves, pts=swap_pts, parts=swap_w, acc=acc, basis=None, total=None, pairs=2)
    return near(
        edges + beyond * leaves,
        pts=relay_pts,
        parts=relay_w,
        acc=acc,
        basis=leaf_basis,
        total=leaf_total,
        pairs=2,
    )


def solution(mesh):
    in_specs = (
        P("leaf", "cols"),
        P("leaf", "cols"),
        P("leaf", None),
        P("leaf", None),
        P("leaf", None),
        P("leaf", None),
        P("leaf", None),
        P(),
        P("leaf", None),
        P("leaf"),
    )
    out_specs = P("leaf", "cols")
    return jax.shard_map(
        per_device, mesh=mesh, in_specs=in_specs, out_specs=out_specs, check_vma=False
    )
```

```python
import functools
import math

import jax
import jax.numpy as jnp
from jax import lax
from jax.experimental import pallas as pl
from jax.experimental.pallas import tpu as pltpu
from jax.sharding import PartitionSpec as P

LEAF = 1024
CHILDREN = 4
SHARPNESS = 2.0
F32 = jnp.float32
BF16 = jnp.bfloat16
VMEM_LIMIT = 48 << 20


def mm(a, b):
    return jnp.dot(a, b, preferred_element_type=F32)


def mm_t(a, b):
    return lax.dot_general(a, b, (((0,), (0,)), ((), ())), preferred_element_type=F32)


def augmented(coords, left):
    wide = coords.astype(F32)
    half = -0.5 * jnp.sum(wide * wide, axis=0, keepdims=True)
    high = half.astype(BF16).astype(F32)
    rest = half - high
    mid = rest.astype(BF16).astype(F32)
    low = rest - mid
    row = lax.broadcasted_iota(jnp.int32, coords.shape, 0)
    at, ones = (0, 3) if left else (3, 0)
    extra = jnp.where((row >= ones) & (row < ones + 3), 1.0, 0.0)
    for k, piece in enumerate((high, mid, low)):
        extra = jnp.where(row == at + k, piece, extra)
    return jnp.concatenate([coords, extra.astype(BF16)], axis=0)


def kernel_of(inner, feat):
    return jnp.exp2(inner * (2.0 * SHARPNESS / feat * math.log2(math.e))).astype(BF16)


def pick(coords, index_row, offset=0):
    n = coords.shape[1]
    place = lax.broadcasted_iota(jnp.int32, (n, index_row.shape[1]), 0)
    hot = jnp.where(place == index_row - offset, 1.0, 0.0).astype(BF16)
    return mm(coords, hot)


def leaf_kernel(
    late, pts_ref, w_ref, basis_ref, dev_ref, group_ref, lskel_ref, dskel_ref,
    field_ref, packed_ref, left_ref, *refs
):
    late_refs, skel_ref = refs[:-1], refs[-1]
    feat = pts_ref.shape[0]
    leaves, rank = lskel_ref.shape
    for ref, l in zip(late_refs, late):
        ref[...] = w_ref[pl.ds(l * LEAF, LEAF), :]
    coords = []
    for l in range(leaves):
        own = pts_ref[:, pl.ds(l * LEAF, LEAF)]
        left_ref[pl.ds(l * LEAF, LEAF), :] = augmented(own, True).T
        skel_ref[pl.ds(l * rank, rank), :] = mm(
            basis_ref[pl.ds(l * rank, rank), :], w_ref[pl.ds(l * LEAF, LEAF), :]
        ).astype(BF16)
        coords.append(pick(own, lskel_ref[pl.ds(l, 1), :]).astype(BF16))
    packed_ref[:rank, :] = mm(dev_ref[...], skel_ref[...]).astype(BF16)
    packed_ref[rank : rank + feat, :] = pick(jnp.concatenate(coords, axis=1), dskel_ref[...]).astype(BF16)
    quarter = group_ref.shape[0]
    for c in range(CHILDREN):
        packed_ref[pl.ds(rank + feat + c * quarter, quarter), :] = group_ref[:, c * rank : (c + 1) * rank]
    rights = [augmented(c, False) for c in coords]
    for l in range(leaves):
        left = augmented(coords[l], True).T
        total = None
        for o in range(leaves):
            if o != l:
                term = mm(kernel_of(mm(left, rights[o]), feat), skel_ref[pl.ds(o * rank, rank), :])
                total = term if total is None else total + term
        field_ref[pl.ds(l * rank, rank), :] = total


def transfer_block(pack, child, rank, feat):
    quarter = rank // CHILDREN
    start = rank + feat
    return pack[pl.ds(pl.multiple_of(start + child * quarter, quarter), quarter), :]


def node_kernel(feat, pos_ref, *refs):
    packs = refs[:CHILDREN]
    gskel_ref, field_ref, group_ref = refs[CHILDREN:]
    member = lax.rem(pos_ref[0], CHILDREN)
    group = pos_ref[0] // CHILDREN
    rank = field_ref.shape[0]
    quarter = rank // CHILDREN
    children = [member ^ f for f in range(CHILDREN)]
    for q in range(CHILDREN):
        total = None
        for f in range(CHILDREN):
            term = mm(transfer_block(packs[q], children[f], rank, feat), packs[f][:rank, :])
            total = term if total is None else total + term
        group_ref[pl.ds(pl.multiple_of(children[q] * quarter, quarter), quarter), :] = total.astype(BF16)
    chosen = gskel_ref[pl.ds(group, 1), :]
    coords = None
    for f in range(CHILDREN):
        term = pick(packs[f][rank : rank + feat, :], chosen, children[f] * rank)
        coords = term if coords is None else coords + term
    group_ref[rank:, :] = coords.astype(BF16)
    left = augmented(packs[0][rank : rank + feat, :], True).T
    total = None
    for f in range(1, CHILDREN):
        inner = mm(left, augmented(packs[f][rank : rank + feat, :], False))
        term = mm(kernel_of(inner, feat), packs[f][:rank, :])
        total = term if total is None else total + term
    field_ref[...] = total


def top_kernel(others, pos_ref, *refs):
    own_ref = refs[0]
    other_refs = refs[1 : 1 + others]
    packs = refs[1 + others : 1 + others + CHILDREN]
    nfield_ref, lfield_ref, dev_ref, out_ref, top_ref = refs[1 + others + CHILDREN :]
    rank = nfield_ref.shape[0]
    feat = own_ref.shape[0] - rank
    quarter = rank // CHILDREN
    member = lax.rem(pos_ref[0], CHILDREN)
    left = augmented(own_ref[rank:, :], True).T
    total = jnp.zeros(nfield_ref.shape, F32)
    for ref in other_refs:
        total += mm(kernel_of(mm(left, augmented(ref[rank:, :], False)), feat), ref[:rank, :])
    top_ref[...] = total.astype(BF16)
    shares = nfield_ref[...]
    for f in range(CHILDREN):
        rows = pl.ds(pl.multiple_of((member ^ f) * quarter, quarter), quarter)
        shares += mm_t(transfer_block(packs[f], member, rank, feat), top_ref[rows, :])
    node_total = shares.astype(BF16)
    out_ref[...] = (lfield_ref[...] + mm_t(dev_ref[...], node_total)).astype(BF16)


def near_kernel(lanes, first, far, info_ref, count_ref, list_ref, *refs):
    refs = list(refs)
    left_ref, pts_ref = refs[:2]
    w_refs = refs[2 : 2 + len(lanes)]
    refs = refs[2 + len(lanes) :]
    acc_ref = None if first else refs.pop(0)
    if far:
        basis_ref, total_ref = refs.pop(0), refs.pop(0)
    (out_ref,) = refs
    leaf = pl.program_id(0)
    feat = pts_ref.shape[0]
    chunk = 256
    if first:
        out_ref[...] = jnp.zeros_like(out_ref)
    elif far:
        out_ref[...] = acc_ref[...] + mm_t(basis_ref[...], total_ref[...])
    else:
        out_ref[...] = acc_ref[...]

    def visit(slot, carry):
        source = list_ref[leaf, slot]
        for part, (lane, w_ref) in enumerate(zip(lanes, w_refs)):
            place = source - info_ref[part]

            @pl.when((place >= 0) & (place < w_ref.shape[0] // LEAF))
            def _():
                at = pl.multiple_of(place * LEAF, LEAF)
                right = augmented(pts_ref[:, pl.ds(pl.multiple_of(lane + at, LEAF), LEAF)], False)
                rows = pl.ds(at, LEAF)
                for r in range(0, LEAF, chunk):
                    block = kernel_of(mm(left_ref[pl.ds(r, chunk), :], right), feat)
                    out_ref[pl.ds(r, chunk), :] += mm(block, w_ref[rows, :])

        return carry

    lax.fori_loop(0, count_ref[leaf], visit, 0)


def whole():
    return pl.BlockSpec(memory_space=pltpu.VMEM)


def scalar():
    return pl.BlockSpec(memory_space=pltpu.SMEM)


def cost(flops, nbytes):
    return pl.CostEstimate(flops=int(flops), bytes_accessed=int(nbytes), transcendentals=0)


def near_call(counts, near_list, left, pts, parts, acc=None, basis=None, total=None, pairs=2):
    arrays = [a for a, _, _ in parts]
    lanes = tuple(n for _, n, _ in parts)
    info = jnp.stack([base for _, _, base in parts]).astype(jnp.int32)
    rows = left.shape[0]
    width = arrays[0].shape[1]
    leaves = rows // LEAF
    const = lambda l, *_: (0, 0)
    args = [left, pts, *arrays]
    block = lambda n, m: pl.BlockSpec((n, m), lambda l, *_: (l, 0))
    specs = [block(LEAF, left.shape[1]), pl.BlockSpec(pts.shape, const)]
    specs += [pl.BlockSpec(p.shape, const) for p in arrays]
    alias = {}
    if acc is not None:
        alias = {3 + len(args): 0}
        args.append(acc)
        specs.append(block(LEAF, width))
    if basis is not None:
        rank = basis.shape[0] // leaves
        args += [basis, total]
        specs += [block(rank, LEAF), block(rank, width)]
    return pl.pallas_call(
        functools.partial(near_kernel, lanes, acc is None, basis is not None),
        grid_spec=pltpu.PrefetchScalarGridSpec(
            num_scalar_prefetch=3,
            grid=(leaves,),
            in_specs=specs,
            out_specs=block(LEAF, width),
        ),
        out_shape=jax.ShapeDtypeStruct((rows, width), F32),
        input_output_aliases=alias,
        compiler_params=pltpu.CompilerParams(vmem_limit_bytes=VMEM_LIMIT),
        cost_estimate=cost(pairs * 1.8e9, 8 << 20),
    )(info, counts, near_list, *args)


def per_device(
    points,
    weights,
    leaf_basis,
    dev_transfer,
    group_transfer,
    leaf_skeleton,
    dev_skeleton,
    group_skeleton,
    near_list,
    near_count,
):
    size = lax.axis_size("leaf")
    position = lax.axis_index("leaf")
    rows, width = weights.shape
    leaves = rows // LEAF
    rank = leaf_skeleton.shape[1]
    groups = size // CHILDREN

    def flipped(value, mask):
        return lax.ppermute(value, "leaf", [(i, i ^ mask) for i in range(size)])

    def relayed(value):
        pairs = [(i, i + 2) for i in range(0, size - 2, 2)]
        pairs += [(i, i - 2) for i in range(3, size, 2)]
        return lax.ppermute(value, "leaf", pairs)

    own_slice = points.T
    swap_slice = flipped(own_slice, 1)
    relay_slice = relayed(swap_slice)
    pts = lax.all_gather(
        jnp.concatenate([own_slice, swap_slice, relay_slice], axis=1), "cols", axis=0, tiled=True
    )
    early = range(leaves // 2)
    late = range(leaves // 2, leaves)
    swap_w = [flipped(weights[l * LEAF : (l + 1) * LEAF], 1) for l in early]
    feat = pts.shape[0]
    params = pltpu.CompilerParams(vmem_limit_bytes=VMEM_LIMIT)
    pack_rows = rank + feat + CHILDREN * group_transfer.shape[0]
    leaf_field, packed, left, *late_w = pl.pallas_call(
        functools.partial(leaf_kernel, tuple(late)),
        out_shape=(
            jax.ShapeDtypeStruct((leaves * rank, width), F32),
            jax.ShapeDtypeStruct((pack_rows, width), BF16),
            jax.ShapeDtypeStruct((rows, 2 * feat), BF16),
        )
        + tuple(jax.ShapeDtypeStruct((LEAF, width), BF16) for _ in late),
        in_specs=[whole()] * 7,
        out_specs=(whole(),) * (3 + len(late)),
        scratch_shapes=[pltpu.VMEM((leaves * rank, width), BF16)],
        compiler_params=params,
        cost_estimate=cost(5e9, 6 << 20),
    )(pts, weights, leaf_basis, dev_transfer, group_transfer, leaf_skeleton, dev_skeleton)
    packs = [packed] + [flipped(packed, f) for f in range(1, CHILDREN)]
    swap_w += [flipped(part, 1) for part in late_w]
    relay_w = [relayed(part) for part in swap_w]

    pos = position.astype(jnp.int32)[None]
    node_field, group = pl.pallas_call(
        functools.partial(node_kernel, feat),
        out_shape=(
            jax.ShapeDtypeStruct((rank, width), F32),
            jax.ShapeDtypeStruct((rank + feat, width), BF16),
        ),
        in_specs=[scalar()] + [whole()] * (CHILDREN + 1),
        out_specs=(whole(), whole()),
        compiler_params=params,
        cost_estimate=cost(2e9, 2 << 20),
    )(pos, *packs, group_skeleton)
    others = [
        lax.ppermute(group, "leaf", [(i, (i + CHILDREN * k) % size) for i in range(size)])
        for k in range(1, groups)
    ]
    leaf_total = pl.pallas_call(
        functools.partial(top_kernel, len(others)),
        out_shape=jax.ShapeDtypeStruct((leaves * rank, width), BF16),
        in_specs=[scalar()] + [whole()] * (len(others) + CHILDREN + 4),
        out_specs=whole(),
        scratch_shapes=[pltpu.VMEM((rank, width), BF16)],
        compiler_params=params,
        cost_estimate=cost(2e9, 3 << 20),
    )(pos, group, *others, *packs, node_field, leaf_field, dev_transfer)

    counts = near_count.astype(jnp.int32)
    beyond = jnp.where(position % 2 == 0, position - 1, position + 1)
    own_part = [(weights, 0, position * leaves)]
    swap_parts = [(w, rows + l * LEAF, (position ^ 1) * leaves + l) for l, w in enumerate(swap_w)]
    relay_parts = [(w, 2 * rows + l * LEAF, beyond * leaves + l) for l, w in enumerate(relay_w)]
    near = functools.partial(near_call, counts, near_list, left, pts)
    half = leaves // 2
    acc = near(own_part + swap_parts[:half], pairs=7)
    acc = near(
        swap_parts[half:] + relay_parts[:half], acc=acc, basis=leaf_basis, total=leaf_total, pairs=5
    )
    return near(relay_parts[half:], acc=acc, pairs=2)


def solution(mesh):
    in_specs = (
        P("leaf", "cols"),
        P("leaf", "cols"),
        P("leaf", None),
        P("leaf", None),
        P("leaf", None),
        P("leaf", None),
        P("leaf", None),
        P(),
        P("leaf", None),
        P("leaf"),
    )
    out_specs = P("leaf", "cols")
    return jax.shard_map(
        per_device, mesh=mesh, in_specs=in_specs, out_specs=out_specs, check_vma=False
    )
```

```python
import functools
import math

import jax
import jax.numpy as jnp
from jax import lax
from jax.experimental import pallas as pl
from jax.experimental.pallas import tpu as pltpu
from jax.sharding import PartitionSpec as P

LEAF = 1024
CHILDREN = 4
SHARPNESS = 2.0
F32 = jnp.float32
BF16 = jnp.bfloat16
VMEM_LIMIT = 48 << 20


def mm(a, b):
    return jnp.dot(a, b, preferred_element_type=F32)


def mm_t(a, b):
    return lax.dot_general(a, b, (((0,), (0,)), ((), ())), preferred_element_type=F32)


def augmented(coords, left):
    wide = coords.astype(F32)
    half = -0.5 * jnp.sum(wide * wide, axis=0, keepdims=True)
    high = half.astype(BF16).astype(F32)
    rest = half - high
    mid = rest.astype(BF16).astype(F32)
    low = rest - mid
    row = lax.broadcasted_iota(jnp.int32, coords.shape, 0)
    at, ones = (0, 3) if left else (3, 0)
    extra = jnp.where((row >= ones) & (row < ones + 3), 1.0, 0.0)
    for k, piece in enumerate((high, mid, low)):
        extra = jnp.where(row == at + k, piece, extra)
    return jnp.concatenate([coords, extra.astype(BF16)], axis=0)


def kernel_of(inner, feat):
    return jnp.exp2(inner * (2.0 * SHARPNESS / feat * math.log2(math.e))).astype(BF16)


def pick(coords, index_row, offset=0):
    n = coords.shape[1]
    place = lax.broadcasted_iota(jnp.int32, (n, index_row.shape[1]), 0)
    hot = jnp.where(place == index_row - offset, 1.0, 0.0).astype(BF16)
    return mm(coords, hot)


def leaf_kernel(
    late, slices, w_ref, basis_ref, dev_ref, group_ref, lskel_ref, dskel_ref, *refs
):
    slice_refs = refs[:slices]
    field_ref, packed_ref, left_ref, pts_ref = refs[slices : slices + 4]
    late_refs, skel_ref = refs[slices + 4 : -1], refs[-1]
    feat = pts_ref.shape[0]
    pts_ref[...] = jnp.concatenate([ref[...] for ref in slice_refs], axis=0)
    leaves, rank = lskel_ref.shape
    for ref, l in zip(late_refs, late):
        ref[...] = w_ref[pl.ds(l * LEAF, LEAF), :]
    coords = []
    for l in range(leaves):
        own = pts_ref[:, pl.ds(l * LEAF, LEAF)]
        left_ref[pl.ds(l * LEAF, LEAF), :] = augmented(own, True).T
        skel_ref[pl.ds(l * rank, rank), :] = mm(
            basis_ref[pl.ds(l * rank, rank), :], w_ref[pl.ds(l * LEAF, LEAF), :]
        ).astype(BF16)
        coords.append(pick(own, lskel_ref[pl.ds(l, 1), :]).astype(BF16))
    packed_ref[:rank, :] = mm(dev_ref[...], skel_ref[...]).astype(BF16)
    packed_ref[rank : rank + feat, :] = pick(jnp.concatenate(coords, axis=1), dskel_ref[...]).astype(BF16)
    quarter = group_ref.shape[0]
    for c in range(CHILDREN):
        packed_ref[pl.ds(rank + feat + c * quarter, quarter), :] = group_ref[:, c * rank : (c + 1) * rank]
    rights = [augmented(c, False) for c in coords]
    for l in range(leaves):
        left = augmented(coords[l], True).T
        total = None
        for o in range(leaves):
            if o != l:
                term = mm(kernel_of(mm(left, rights[o]), feat), skel_ref[pl.ds(o * rank, rank), :])
                total = term if total is None else total + term
        field_ref[pl.ds(l * rank, rank), :] = total


def transfer_block(pack, child, rank, feat):
    quarter = rank // CHILDREN
    start = rank + feat
    return pack[pl.ds(pl.multiple_of(start + child * quarter, quarter), quarter), :]


def node_kernel(feat, pos_ref, *refs):
    packs = refs[:CHILDREN]
    gskel_ref, field_ref, group_ref = refs[CHILDREN:]
    member = lax.rem(pos_ref[0], CHILDREN)
    group = pos_ref[0] // CHILDREN
    rank = field_ref.shape[0]
    quarter = rank // CHILDREN
    children = [member ^ f for f in range(CHILDREN)]
    for q in range(CHILDREN):
        total = None
        for f in range(CHILDREN):
            term = mm(transfer_block(packs[q], children[f], rank, feat), packs[f][:rank, :])
            total = term if total is None else total + term
        group_ref[pl.ds(pl.multiple_of(children[q] * quarter, quarter), quarter), :] = total.astype(BF16)
    chosen = gskel_ref[pl.ds(group, 1), :]
    coords = None
    for f in range(CHILDREN):
        term = pick(packs[f][rank : rank + feat, :], chosen, children[f] * rank)
        coords = term if coords is None else coords + term
    group_ref[rank:, :] = coords.astype(BF16)
    left = augmented(packs[0][rank : rank + feat, :], True).T
    total = None
    for f in range(1, CHILDREN):
        inner = mm(left, augmented(packs[f][rank : rank + feat, :], False))
        term = mm(kernel_of(inner, feat), packs[f][:rank, :])
        total = term if total is None else total + term
    field_ref[...] = total


def top_kernel(others, pos_ref, *refs):
    own_ref = refs[0]
    other_refs = refs[1 : 1 + others]
    packs = refs[1 + others : 1 + others + CHILDREN]
    nfield_ref, lfield_ref, dev_ref, out_ref, top_ref = refs[1 + others + CHILDREN :]
    rank = nfield_ref.shape[0]
    feat = own_ref.shape[0] - rank
    quarter = rank // CHILDREN
    member = lax.rem(pos_ref[0], CHILDREN)
    left = augmented(own_ref[rank:, :], True).T
    total = jnp.zeros(nfield_ref.shape, F32)
    for ref in other_refs:
        total += mm(kernel_of(mm(left, augmented(ref[rank:, :], False)), feat), ref[:rank, :])
    top_ref[...] = total.astype(BF16)
    shares = nfield_ref[...]
    for f in range(CHILDREN):
        rows = pl.ds(pl.multiple_of((member ^ f) * quarter, quarter), quarter)
        shares += mm_t(transfer_block(packs[f], member, rank, feat), top_ref[rows, :])
    node_total = shares.astype(BF16)
    out_ref[...] = (lfield_ref[...] + mm_t(dev_ref[...], node_total)).astype(BF16)


def near_kernel(lanes, slices, first, far, info_ref, count_ref, list_ref, *refs):
    refs = list(refs)
    left_ref, own_ref = refs[:2]
    halo_refs = refs[2 : 2 + slices]
    refs = refs[2 + slices :]
    w_refs = refs[: len(lanes)]
    refs = refs[len(lanes) :]
    acc_ref = None if first else refs.pop(0)
    if far:
        basis_ref, total_ref = refs.pop(0), refs.pop(0)
    (out_ref,) = refs
    leaf = pl.program_id(0)
    feat = own_ref.shape[0]
    chunk = 256
    if first:
        out_ref[...] = jnp.zeros_like(out_ref)
    elif far:
        out_ref[...] = acc_ref[...] + mm_t(basis_ref[...], total_ref[...])
    else:
        out_ref[...] = acc_ref[...]

    def visit(slot, carry):
        source = list_ref[leaf, slot]
        for part, (lane, w_ref) in enumerate(zip(lanes, w_refs)):
            place = source - info_ref[part]

            @pl.when((place >= 0) & (place < w_ref.shape[0] // LEAF))
            def _():
                at = pl.multiple_of(place * LEAF, LEAF)
                if lane is None:
                    coords = own_ref[:, pl.ds(at, LEAF)]
                else:
                    cols = pl.ds(pl.multiple_of(lane + at, LEAF), LEAF)
                    coords = jnp.concatenate([ref[:, cols] for ref in halo_refs], axis=0)
                right = augmented(coords, False)
                rows = pl.ds(at, LEAF)
                for r in range(0, LEAF, chunk):
                    block = kernel_of(mm(left_ref[pl.ds(r, chunk), :], right), feat)
                    out_ref[pl.ds(r, chunk), :] += mm(block, w_ref[rows, :])

        return carry

    lax.fori_loop(0, count_ref[leaf], visit, 0)


def whole():
    return pl.BlockSpec(memory_space=pltpu.VMEM)


def scalar():
    return pl.BlockSpec(memory_space=pltpu.SMEM)


def cost(flops, nbytes):
    return pl.CostEstimate(flops=int(flops), bytes_accessed=int(nbytes), transcendentals=0)


def near_call(counts, near_list, left, own_pts, halo_pts, parts, acc=None, basis=None, total=None, pairs=2):
    arrays = [a for a, _, _ in parts]
    lanes = tuple(n for _, n, _ in parts)
    info = jnp.stack([base for _, _, base in parts]).astype(jnp.int32)
    rows = left.shape[0]
    width = arrays[0].shape[1]
    leaves = rows // LEAF
    const = lambda l, *_: (0, 0)
    args = [left, own_pts, *halo_pts, *arrays]
    block = lambda n, m: pl.BlockSpec((n, m), lambda l, *_: (l, 0))
    specs = [block(LEAF, left.shape[1])]
    specs += [pl.BlockSpec(p.shape, const) for p in args[1:]]
    alias = {}
    if acc is not None:
        alias = {3 + len(args): 0}
        args.append(acc)
        specs.append(block(LEAF, width))
    if basis is not None:
        rank = basis.shape[0] // leaves
        args += [basis, total]
        specs += [block(rank, LEAF), block(rank, width)]
    return pl.pallas_call(
        functools.partial(near_kernel, lanes, len(halo_pts), acc is None, basis is not None),
        grid_spec=pltpu.PrefetchScalarGridSpec(
            num_scalar_prefetch=3,
            grid=(leaves,),
            in_specs=specs,
            out_specs=block(LEAF, width),
        ),
        out_shape=jax.ShapeDtypeStruct((rows, width), F32),
        input_output_aliases=alias,
        compiler_params=pltpu.CompilerParams(vmem_limit_bytes=VMEM_LIMIT),
        cost_estimate=cost(pairs * 1.8e9, 8 << 20),
    )(info, counts, near_list, *args)


def per_device(
    points,
    weights,
    leaf_basis,
    dev_transfer,
    group_transfer,
    leaf_skeleton,
    dev_skeleton,
    group_skeleton,
    near_list,
    near_count,
):
    size = lax.axis_size("leaf")
    position = lax.axis_index("leaf")
    rows, width = weights.shape
    leaves = rows // LEAF
    rank = leaf_skeleton.shape[1]
    groups = size // CHILDREN

    def flipped(value, mask):
        return lax.ppermute(value, "leaf", [(i, i ^ mask) for i in range(size)])

    def relayed(value):
        pairs = [(i, i + 2) for i in range(0, size - 2, 2)]
        pairs += [(i, i - 2) for i in range(3, size, 2)]
        return lax.ppermute(value, "leaf", pairs)

    def over_cols(value):
        count = lax.axis_size("cols")
        return [value] + [
            lax.ppermute(value, "cols", [(i, i ^ f) for i in range(count)]) for f in range(1, count)
        ]

    own_slice = points.T
    own_slices = over_cols(own_slice)
    swap_slice = flipped(own_slice, 1)
    relay_slice = relayed(swap_slice)
    halo_pts = over_cols(jnp.concatenate([swap_slice, relay_slice], axis=1))
    early = range(1)
    late = range(1, leaves)
    swap_w = [flipped(weights[l * LEAF : (l + 1) * LEAF], 1) for l in early]
    feat = sum(part.shape[0] for part in own_slices)
    params = pltpu.CompilerParams(vmem_limit_bytes=VMEM_LIMIT)
    pack_rows = rank + feat + CHILDREN * group_transfer.shape[0]
    leaf_field, packed, left, own_pts, *late_w = pl.pallas_call(
        functools.partial(leaf_kernel, tuple(late), len(own_slices)),
        out_shape=(
            jax.ShapeDtypeStruct((leaves * rank, width), F32),
            jax.ShapeDtypeStruct((pack_rows, width), BF16),
            jax.ShapeDtypeStruct((rows, 2 * feat), BF16),
            jax.ShapeDtypeStruct((feat, rows), BF16),
        )
        + tuple(jax.ShapeDtypeStruct((LEAF, width), BF16) for _ in late),
        in_specs=[whole()] * (6 + len(own_slices)),
        out_specs=(whole(),) * (4 + len(late)),
        scratch_shapes=[pltpu.VMEM((leaves * rank, width), BF16)],
        compiler_params=params,
        cost_estimate=cost(5e9, 6 << 20),
    )(weights, leaf_basis, dev_transfer, group_transfer, leaf_skeleton, dev_skeleton, *own_slices)
    packs = [packed] + [flipped(packed, f) for f in range(1, CHILDREN)]
    swap_w += [flipped(part, 1) for part in late_w]
    relay_w = [relayed(part) for part in swap_w]

    pos = position.astype(jnp.int32)[None]
    node_field, group = pl.pallas_call(
        functools.partial(node_kernel, feat),
        out_shape=(
            jax.ShapeDtypeStruct((rank, width), F32),
            jax.ShapeDtypeStruct((rank + feat, width), BF16),
        ),
        in_specs=[scalar()] + [whole()] * (CHILDREN + 1),
        out_specs=(whole(), whole()),
        compiler_params=params,
        cost_estimate=cost(2e9, 2 << 20),
    )(pos, *packs, group_skeleton)
    others = [
        lax.ppermute(group, "leaf", [(i, (i + CHILDREN * k) % size) for i in range(size)])
        for k in range(1, groups)
    ]
    leaf_total = pl.pallas_call(
        functools.partial(top_kernel, len(others)),
        out_shape=jax.ShapeDtypeStruct((leaves * rank, width), BF16),
        in_specs=[scalar()] + [whole()] * (len(others) + CHILDREN + 4),
        out_specs=whole(),
        scratch_shapes=[pltpu.VMEM((rank, width), BF16)],
        compiler_params=params,
        cost_estimate=cost(2e9, 3 << 20),
    )(pos, group, *others, *packs, node_field, leaf_field, dev_transfer)

    counts = near_count.astype(jnp.int32)
    beyond = jnp.where(position % 2 == 0, position - 1, position + 1)
    own_part = [(weights, None, position * leaves)]
    swap_parts = [(w, l * LEAF, (position ^ 1) * leaves + l) for l, w in enumerate(swap_w)]
    relay_parts = [(w, rows + l * LEAF, beyond * leaves + l) for l, w in enumerate(relay_w)]
    near = functools.partial(near_call, counts, near_list, left, own_pts, halo_pts)
    half = leaves // 2
    acc = near(own_part + swap_parts[:1], pairs=6)
    acc = near(
        swap_parts[1:] + relay_parts[:half], acc=acc, basis=leaf_basis, total=leaf_total, pairs=5
    )
    return near(relay_parts[half:], acc=acc, pairs=2)


def solution(mesh):
    in_specs = (
        P("leaf", "cols"),
        P("leaf", "cols"),
        P("leaf", None),
        P("leaf", None),
        P("leaf", None),
        P("leaf", None),
        P("leaf", None),
        P(),
        P("leaf", None),
        P("leaf"),
    )
    out_specs = P("leaf", "cols")
    return jax.shard_map(
        per_device, mesh=mesh, in_specs=in_specs, out_specs=out_specs, check_vma=False
    )
```

```python
import functools
import math

import jax
import jax.numpy as jnp
from jax import lax
from jax.experimental import pallas as pl
from jax.experimental.pallas import tpu as pltpu
from jax.sharding import PartitionSpec as P

LEAF = 1024
CHILDREN = 4
SHARPNESS = 2.0
F32 = jnp.float32
BF16 = jnp.bfloat16
VMEM_LIMIT = 48 << 20


def mm(a, b):
    return jnp.dot(a, b, preferred_element_type=F32)


def mm_t(a, b):
    return lax.dot_general(a, b, (((0,), (0,)), ((), ())), preferred_element_type=F32)


def augmented(coords, left):
    wide = coords.astype(F32)
    half = -0.5 * jnp.sum(wide * wide, axis=0, keepdims=True)
    high = half.astype(BF16).astype(F32)
    rest = half - high
    mid = rest.astype(BF16).astype(F32)
    low = rest - mid
    row = lax.broadcasted_iota(jnp.int32, coords.shape, 0)
    at, ones = (0, 3) if left else (3, 0)
    extra = jnp.where((row >= ones) & (row < ones + 3), 1.0, 0.0)
    for k, piece in enumerate((high, mid, low)):
        extra = jnp.where(row == at + k, piece, extra)
    return jnp.concatenate([coords, extra.astype(BF16)], axis=0)


def kernel_of(inner, feat):
    return jnp.exp2(inner * (2.0 * SHARPNESS / feat * math.log2(math.e))).astype(BF16)


def pick(coords, index_row, offset=0):
    n = coords.shape[1]
    place = lax.broadcasted_iota(jnp.int32, (n, index_row.shape[1]), 0)
    hot = jnp.where(place == index_row - offset, 1.0, 0.0).astype(BF16)
    return mm(coords, hot)


def leaf_kernel(
    late, slices, w_ref, basis_ref, dev_ref, group_ref, lskel_ref, dskel_ref, *refs
):
    slice_refs = refs[:slices]
    field_ref, packed_ref, left_ref, pts_ref = refs[slices : slices + 4]
    late_refs, skel_ref = refs[slices + 4 : -1], refs[-1]
    feat = pts_ref.shape[0]
    pts_ref[...] = jnp.concatenate([ref[...] for ref in slice_refs], axis=0)
    leaves, rank = lskel_ref.shape
    for ref, l in zip(late_refs, late):
        ref[...] = w_ref[pl.ds(l * LEAF, LEAF), :]
    coords = []
    for l in range(leaves):
        own = pts_ref[:, pl.ds(l * LEAF, LEAF)]
        left_ref[pl.ds(l * LEAF, LEAF), :] = augmented(own, True).T
        skel_ref[pl.ds(l * rank, rank), :] = mm(
            basis_ref[pl.ds(l * rank, rank), :], w_ref[pl.ds(l * LEAF, LEAF), :]
        ).astype(BF16)
        coords.append(pick(own, lskel_ref[pl.ds(l, 1), :]).astype(BF16))
    packed_ref[:rank, :] = mm(dev_ref[...], skel_ref[...]).astype(BF16)
    packed_ref[rank : rank + feat, :] = pick(jnp.concatenate(coords, axis=1), dskel_ref[...]).astype(BF16)
    quarter = group_ref.shape[0]
    for c in range(CHILDREN):
        packed_ref[pl.ds(rank + feat + c * quarter, quarter), :] = group_ref[:, c * rank : (c + 1) * rank]
    rights = [augmented(c, False) for c in coords]
    for l in range(leaves):
        left = augmented(coords[l], True).T
        total = None
        for o in range(leaves):
            if o != l:
                term = mm(kernel_of(mm(left, rights[o]), feat), skel_ref[pl.ds(o * rank, rank), :])
                total = term if total is None else total + term
        field_ref[pl.ds(l * rank, rank), :] = total


def transfer_block(pack, child, rank, feat):
    quarter = rank // CHILDREN
    start = rank + feat
    return pack[pl.ds(pl.multiple_of(start + child * quarter, quarter), quarter), :]


def node_kernel(feat, pos_ref, *refs):
    packs = refs[:CHILDREN]
    gskel_ref, field_ref, group_ref = refs[CHILDREN:]
    member = lax.rem(pos_ref[0], CHILDREN)
    group = pos_ref[0] // CHILDREN
    rank = field_ref.shape[0]
    quarter = rank // CHILDREN
    children = [member ^ f for f in range(CHILDREN)]
    for q in range(CHILDREN):
        total = None
        for f in range(CHILDREN):
            term = mm(transfer_block(packs[q], children[f], rank, feat), packs[f][:rank, :])
            total = term if total is None else total + term
        group_ref[pl.ds(pl.multiple_of(children[q] * quarter, quarter), quarter), :] = total.astype(BF16)
    chosen = gskel_ref[pl.ds(group, 1), :]
    coords = None
    for f in range(CHILDREN):
        term = pick(packs[f][rank : rank + feat, :], chosen, children[f] * rank)
        coords = term if coords is None else coords + term
    group_ref[rank:, :] = coords.astype(BF16)
    left = augmented(packs[0][rank : rank + feat, :], True).T
    total = None
    for f in range(1, CHILDREN):
        inner = mm(left, augmented(packs[f][rank : rank + feat, :], False))
        term = mm(kernel_of(inner, feat), packs[f][:rank, :])
        total = term if total is None else total + term
    field_ref[...] = total


def top_kernel(others, pos_ref, *refs):
    own_ref = refs[0]
    other_refs = refs[1 : 1 + others]
    packs = refs[1 + others : 1 + others + CHILDREN]
    nfield_ref, lfield_ref, dev_ref, out_ref, top_ref = refs[1 + others + CHILDREN :]
    rank = nfield_ref.shape[0]
    feat = own_ref.shape[0] - rank
    quarter = rank // CHILDREN
    member = lax.rem(pos_ref[0], CHILDREN)
    left = augmented(own_ref[rank:, :], True).T
    total = jnp.zeros(nfield_ref.shape, F32)
    for ref in other_refs:
        total += mm(kernel_of(mm(left, augmented(ref[rank:, :], False)), feat), ref[:rank, :])
    top_ref[...] = total.astype(BF16)
    shares = nfield_ref[...]
    for f in range(CHILDREN):
        rows = pl.ds(pl.multiple_of((member ^ f) * quarter, quarter), quarter)
        shares += mm_t(transfer_block(packs[f], member, rank, feat), top_ref[rows, :])
    node_total = shares.astype(BF16)
    out_ref[...] = (lfield_ref[...] + mm_t(dev_ref[...], node_total)).astype(BF16)


def near_kernel(lanes, slices, first, far, info_ref, count_ref, list_ref, *refs):
    refs = list(refs)
    left_ref, own_ref = refs[:2]
    halo_refs = refs[2 : 2 + slices]
    refs = refs[2 + slices :]
    w_refs = refs[: len(lanes)]
    refs = refs[len(lanes) :]
    acc_ref = None if first else refs.pop(0)
    if far:
        basis_ref, total_ref = refs.pop(0), refs.pop(0)
    (out_ref,) = refs
    leaf = pl.program_id(0)
    feat = own_ref.shape[0]
    chunk = 256
    if first:
        out_ref[...] = jnp.zeros_like(out_ref)
    elif far:
        out_ref[...] = acc_ref[...] + mm_t(basis_ref[...], total_ref[...])
    else:
        out_ref[...] = acc_ref[...]

    def visit(slot, carry):
        source = list_ref[leaf, slot]
        for part, (lane, w_ref) in enumerate(zip(lanes, w_refs)):
            place = source - info_ref[part]

            @pl.when((place >= 0) & (place < w_ref.shape[0] // LEAF))
            def _():
                at = pl.multiple_of(place * LEAF, LEAF)
                if lane is None:
                    coords = own_ref[:, pl.ds(at, LEAF)]
                else:
                    cols = pl.ds(pl.multiple_of(lane + at, LEAF), LEAF)
                    coords = jnp.concatenate([ref[:, cols] for ref in halo_refs], axis=0)
                right = augmented(coords, False)
                rows = pl.ds(at, LEAF)
                for r in range(0, LEAF, chunk):
                    block = kernel_of(mm(left_ref[pl.ds(r, chunk), :], right), feat)
                    out_ref[pl.ds(r, chunk), :] += mm(block, w_ref[rows, :])

        return carry

    lax.fori_loop(0, count_ref[leaf], visit, 0)


def whole():
    return pl.BlockSpec(memory_space=pltpu.VMEM)


def scalar():
    return pl.BlockSpec(memory_space=pltpu.SMEM)


def cost(flops, nbytes):
    return pl.CostEstimate(flops=int(flops), bytes_accessed=int(nbytes), transcendentals=0)


def near_call(counts, near_list, left, own_pts, halo_pts, parts, acc=None, basis=None, total=None, pairs=2):
    arrays = [a for a, _, _ in parts]
    lanes = tuple(n for _, n, _ in parts)
    info = jnp.stack([base for _, _, base in parts]).astype(jnp.int32)
    rows = left.shape[0]
    width = arrays[0].shape[1]
    leaves = rows // LEAF
    const = lambda l, *_: (0, 0)
    args = [left, own_pts, *halo_pts, *arrays]
    block = lambda n, m: pl.BlockSpec((n, m), lambda l, *_: (l, 0))
    specs = [block(LEAF, left.shape[1])]
    specs += [pl.BlockSpec(p.shape, const) for p in args[1:]]
    alias = {}
    if acc is not None:
        alias = {3 + len(args): 0}
        args.append(acc)
        specs.append(block(LEAF, width))
    if basis is not None:
        rank = basis.shape[0] // leaves
        args += [basis, total]
        specs += [block(rank, LEAF), block(rank, width)]
    return pl.pallas_call(
        functools.partial(near_kernel, lanes, len(halo_pts), acc is None, basis is not None),
        grid_spec=pltpu.PrefetchScalarGridSpec(
            num_scalar_prefetch=3,
            grid=(leaves,),
            in_specs=specs,
            out_specs=block(LEAF, width),
        ),
        out_shape=jax.ShapeDtypeStruct((rows, width), F32),
        input_output_aliases=alias,
        compiler_params=pltpu.CompilerParams(vmem_limit_bytes=VMEM_LIMIT),
        cost_estimate=cost(pairs * 1.8e9, 8 << 20),
    )(info, counts, near_list, *args)


def per_device(
    points,
    weights,
    leaf_basis,
    dev_transfer,
    group_transfer,
    leaf_skeleton,
    dev_skeleton,
    group_skeleton,
    near_list,
    near_count,
):
    size = lax.axis_size("leaf")
    position = lax.axis_index("leaf")
    rows, width = weights.shape
    leaves = rows // LEAF
    rank = leaf_skeleton.shape[1]
    groups = size // CHILDREN

    def flipped(value, mask):
        return lax.ppermute(value, "leaf", [(i, i ^ mask) for i in range(size)])

    def relayed(value):
        pairs = [(i, i + 2) for i in range(0, size - 2, 2)]
        pairs += [(i, i - 2) for i in range(3, size, 2)]
        return lax.ppermute(value, "leaf", pairs)

    def over_cols(value):
        count = lax.axis_size("cols")
        return [value] + [
            lax.ppermute(value, "cols", [(i, i ^ f) for i in range(count)]) for f in range(1, count)
        ]

    own_slice = points.T
    own_slices = over_cols(own_slice)
    swap_slice = flipped(own_slice, 1)
    relay_slice = relayed(swap_slice)
    halo_pts = over_cols(jnp.concatenate([swap_slice, relay_slice], axis=1))
    early = range(leaves // 2)
    late = range(leaves // 2, leaves)
    swap_w = [flipped(weights[l * LEAF : (l + 1) * LEAF], 1) for l in early]
    feat = sum(part.shape[0] for part in own_slices)
    params = pltpu.CompilerParams(vmem_limit_bytes=VMEM_LIMIT)
    pack_rows = rank + feat + CHILDREN * group_transfer.shape[0]
    leaf_field, packed, left, own_pts, *late_w = pl.pallas_call(
        functools.partial(leaf_kernel, tuple(late), len(own_slices)),
        out_shape=(
            jax.ShapeDtypeStruct((leaves * rank, width), F32),
            jax.ShapeDtypeStruct((pack_rows, width), BF16),
            jax.ShapeDtypeStruct((rows, 2 * feat), BF16),
            jax.ShapeDtypeStruct((feat, rows), BF16),
        )
        + tuple(jax.ShapeDtypeStruct((LEAF, width), BF16) for _ in late),
        in_specs=[whole()] * (6 + len(own_slices)),
        out_specs=(whole(),) * (4 + len(late)),
        scratch_shapes=[pltpu.VMEM((leaves * rank, width), BF16)],
        compiler_params=params,
        cost_estimate=cost(5e9, 6 << 20),
    )(weights, leaf_basis, dev_transfer, group_transfer, leaf_skeleton, dev_skeleton, *own_slices)
    packs = [packed] + [flipped(packed, f) for f in range(1, CHILDREN)]
    swap_w += [flipped(part, 1) for part in late_w]
    relay_w = [relayed(part) for part in swap_w]

    pos = position.astype(jnp.int32)[None]
    node_field, group = pl.pallas_call(
        functools.partial(node_kernel, feat),
        out_shape=(
            jax.ShapeDtypeStruct((rank, width), F32),
            jax.ShapeDtypeStruct((rank + feat, width), BF16),
        ),
        in_specs=[scalar()] + [whole()] * (CHILDREN + 1),
        out_specs=(whole(), whole()),
        compiler_params=params,
        cost_estimate=cost(2e9, 2 << 20),
    )(pos, *packs, group_skeleton)
    others = [
        lax.ppermute(group, "leaf", [(i, (i + CHILDREN * k) % size) for i in range(size)])
        for k in range(1, groups)
    ]
    leaf_total = pl.pallas_call(
        functools.partial(top_kernel, len(others)),
        out_shape=jax.ShapeDtypeStruct((leaves * rank, width), BF16),
        in_specs=[scalar()] + [whole()] * (len(others) + CHILDREN + 4),
        out_specs=whole(),
        scratch_shapes=[pltpu.VMEM((rank, width), BF16)],
        compiler_params=params,
        cost_estimate=cost(2e9, 3 << 20),
    )(pos, group, *others, *packs, node_field, leaf_field, dev_transfer)

    counts = near_count.astype(jnp.int32)
    beyond = jnp.where(position % 2 == 0, position - 1, position + 1)
    own_part = [(weights, None, position * leaves)]
    swap_parts = [(w, l * LEAF, (position ^ 1) * leaves + l) for l, w in enumerate(swap_w)]
    relay_parts = [(w, rows + l * LEAF, beyond * leaves + l) for l, w in enumerate(relay_w)]
    near = functools.partial(near_call, counts, near_list, left, own_pts, halo_pts)
    half = leaves // 2
    acc = near(own_part + swap_parts[:1], pairs=6)
    acc = near(
        swap_parts[1:] + relay_parts[:half], acc=acc, basis=leaf_basis, total=leaf_total, pairs=5
    )
    return near(relay_parts[half:], acc=acc, pairs=2)


def solution(mesh):
    in_specs = (
        P("leaf", "cols"),
        P("leaf", "cols"),
        P("leaf", None),
        P("leaf", None),
        P("leaf", None),
        P("leaf", None),
        P("leaf", None),
        P(),
        P("leaf", None),
        P("leaf"),
    )
    out_specs = P("leaf", "cols")
    return jax.shard_map(
        per_device, mesh=mesh, in_specs=in_specs, out_specs=out_specs, check_vma=False
    )
```
